512 devices in a mesh: expert: 64 (over z, y_lo, core), tensor: 8 (over y_hi, x).
Axes of the slice: x: 4, y: 4 (y_hi: 2, y_lo: 2; y = y_hi * 2 + y_lo), z: 16, core: 2. Of those that a mesh axis runs over, the one named last changes fastest.
Arguments:
- tokens: bfloat16 [16384, 2048], P('expert', 'tensor'), may hold values from -6 to 6
- gate_values: float32 [16384, 2], P('expert'), may hold values from 0.25 to 1
- expert_ids: int32 [16384, 2], P('expert'), may hold values from 0 to 63, as said below
- slot_index: int32 [16384, 2], P('expert'), may hold values from -1 to 9, as said below
- w_in: bfloat16 [64, 2048, 4096], P('expert', None, 'tensor'), may hold values from -0.125 to 0.125
- w_out: bfloat16 [64, 4096, 2048], P('expert', 'tensor'), may hold values from -0.09375 to 0.09375
Outputs:
- combined: bfloat16 [16384, 2048], P('expert', 'tensor')
The draws below stay inside these ranges and needn't reach their ends.
Inputs may be any that keep to these rules, and one draw needn't show every extreme that they name: `expert_ids`: the 2 experts of a token differ. `slot_index`: within each source block of 256 tokens, with choices taken in order of token and then of choice, the i-th choice of an expert (i from 0) has slot i if i < 10 and -1 otherwise.
All inputs are finite; a program needn't handle non-finite values.
Results may differ from the reference program's by a relative error of at most 0.019.
Values may be sent and summed in bfloat16 or wider, within the bound.
A program may use at most 64 MiB of HBM per device.

```python
import jax
import jax.numpy as jnp
from jax import lax

D = 2048
FF = 4096
TOP = 2
TOK_DEV = 256
EXPERTS = 64
TOKENS = 16384
CAP = 10
N_EXPERT = 64
N_TENSOR = 8


def routing(key):
    hot_key, first_key, pick_key, second_key = jax.random.split(key, 4)
    hot_expert = jax.random.randint(hot_key, (), 0, EXPERTS)
    random_first = jax.random.randint(first_key, (TOKENS,), 0, EXPERTS)
    pick_hot = jax.random.randint(pick_key, (TOKENS,), 0, 3)
    first_choice = jnp.where(pick_hot == 0, hot_expert, random_first)
    offset = jax.random.randint(second_key, (TOKENS,), 1, EXPERTS)
    second_choice = (first_choice + offset) % EXPERTS
    chosen = jnp.stack([first_choice, second_choice], axis=1).astype(jnp.int32)
    matches = (chosen[:, :, None] == jnp.arange(EXPERTS, dtype=jnp.int32)).astype(jnp.int32)
    flat_hits = matches.reshape(TOKENS // TOK_DEV, TOK_DEV * TOP, EXPERTS)
    earlier = jnp.cumsum(flat_hits, axis=1) - flat_hits
    position = jnp.sum(earlier * flat_hits, axis=2).reshape(TOKENS, TOP)
    slot_values = jnp.where(position < CAP, position, -1).astype(jnp.int32)
    return (chosen, slot_values)


def draw_expert_ids(key, part):
    return routing(key)[0]


def draw_slot_index(key, part):
    return routing(key)[1]


def shard_levels(stream_key, extent, cuts, least, top_value):
    gain = 1.0
    for dim, parts in cuts:
        steps = jax.random.uniform(jax.random.fold_in(jax.random.fold_in(stream_key, 6), dim), (parts,), jnp.float32, least / len(cuts), top_value / len(cuts))
        gain = gain * jnp.repeat(jnp.exp(steps), extent[dim] // parts).reshape((-1,) + (1,) * (len(extent) - 1 - dim))
    return gain


def normal_values(rng, dims, deviation, limit, cuts=(), kind=jnp.bfloat16):
    drawn = deviation * jax.random.normal(rng, dims, jnp.float32)
    if cuts:
        drawn = drawn * shard_levels(rng, dims, cuts, -0.22, 0.18)
    return jnp.clip(drawn, -limit, limit).astype(kind)


def setup_inputs(seed: int = 0) -> dict:
    seeds = jax.random.split(jax.random.key(seed), 7)
    return {
        "tokens": normal_values(seeds[0], (TOKENS, D), 1.0, 6.0, ((0, 64), (1, 8))),
        "gate_values": jnp.clip(0.25 + 0.75 * jax.random.uniform(seeds[1], (TOKENS, TOP), jnp.float32) ** shard_levels(seeds[1], (TOKENS, TOP), ((0, 64),), -0.2, 0.2), 0.25, 1.0),
        "expert_ids": draw_expert_ids(jax.random.fold_in(seeds[6], 71), 0),
        "slot_index": draw_slot_index(jax.random.fold_in(seeds[6], 71), 0),
        "w_in": normal_values(seeds[4], (EXPERTS, D, FF), D ** -0.5, 0.125, ((0, 64), (2, 8))),
        "w_out": normal_values(seeds[5], (EXPERTS, FF, D), FF ** -0.5, 0.09375, ((0, 64), (1, 8))),
    }


def reference(tokens, gate_values, expert_ids, slot_index, w_in, w_out):
    sources = N_EXPERT
    panel_rows = sources * CAP
    unit_count = FF // N_TENSOR
    token_ids = jnp.arange(TOKENS, dtype=jnp.int32)
    source_block = token_ids // TOK_DEV
    is_kept = slot_index >= 0
    where_row = (expert_ids * sources + source_block[:, None]) * CAP + slot_index
    dump_row = EXPERTS * panel_rows
    target = jnp.where(is_kept, where_row, dump_row).astype(jnp.int32)
    row_table = jnp.full((dump_row + 1,), TOKENS, jnp.int32)
    row_table = row_table.at[target.reshape(-1)].set(jnp.repeat(token_ids, TOP).astype(jnp.int32))
    row_table = row_table[:dump_row].reshape(EXPERTS, panel_rows)
    padded = jnp.concatenate([tokens, jnp.zeros((1, D), tokens.dtype)], axis=0)

    def one_expert(inputs):
        row_numbers, weight_in, weight_out = inputs
        panel_in = jnp.take(padded, row_numbers, axis=0)
        pre_act = jnp.dot(panel_in, weight_in, preferred_element_type=jnp.float32)
        hidden = jax.nn.gelu(pre_act, approximate=True).astype(jnp.bfloat16)
        hidden_split = hidden.reshape(panel_rows, N_TENSOR, unit_count).transpose(1, 0, 2).astype(jnp.float32)
        out_split = weight_out.reshape(N_TENSOR, unit_count, D).astype(jnp.float32)
        partial_value = jnp.einsum("jru,jud->jrd", hidden_split, out_split, precision=lax.Precision.HIGHEST).astype(jnp.bfloat16)
        return jnp.sum(partial_value.astype(jnp.float32), axis=0).astype(jnp.bfloat16)

    expert_out = lax.map(one_expert, (row_table, w_in, w_out)).reshape(dump_row, D)
    safe_rows = jnp.where(is_kept, target, 0).astype(jnp.int32)
    weight = jnp.where(is_kept, gate_values, 0.0).astype(jnp.float32)
    first_pick = jnp.take(expert_out, safe_rows[:, 0], axis=0).astype(jnp.float32)
    second_pick = jnp.take(expert_out, safe_rows[:, 1], axis=0).astype(jnp.float32)
    combined = weight[:, 0:1] * first_pick + weight[:, 1:2] * second_pick
    return combined.astype(jnp.bfloat16)
```

```python
import functools

import jax
import jax.numpy as jnp
from jax import lax
from jax.experimental import pallas as pl
from jax.experimental.pallas import tpu as pltpu
from jax.sharding import PartitionSpec as P

MESH = pl.DeviceIdType.MESH
BF, F32 = jnp.bfloat16, jnp.float32

NZ = 16
SUB = 4
CAP = 10
PEERS = 8
UNIT = SUB * CAP
DZ = (0, 2, 1, -2, -1, 4, 3, -4, -3, 6, 5, -6, -5, 7, 8, -7)
SLOT_OF = {d % NZ: k for k, d in enumerate(DZ)}
BACK = tuple(SLOT_OF[(-d) % NZ] for d in DZ)
GROUPS = 4
PER = NZ // GROUPS
OFFS = tuple((h, x) for h in range(2) for x in range(4))
OFF_BACK = tuple(OFFS.index((h, (-x) % 4)) for h, x in OFFS)


def places():
    e, t = lax.axis_index("expert"), lax.axis_index("tensor")
    return e // 4, (e // 2) % 2, e % 2, t // 4, t % 4


def kernel(tok, ids, slot, gate, w_in, w_out, out,
           w1, w2, mix, unmix, gates_hi, gates_lo,
           near_out, near_in, far_out, far_in, part_out, part_in,
           back_out, back_in, last_out, last_in,
           w_sem, near_s, near_r, far_s, far_r, ag_s, ag_r, rs_s, rs_r,
           back_s, back_r, last_s, last_r):
    z, ylo, core, yhi, x = places()
    tens = yhi * 4 + x

    def at_sub(i):
        return (z * 4 + ((ylo + i // 2) % 2) * 2 + (core + i % 2) % 2, tens)

    def at_z(d):
        return (((z + d + NZ) % NZ) * 4 + ylo * 2 + core, tens)

    def peer_index(r):
        h, dx = OFFS[r]
        return ((yhi + h) % 2) * 4 + (x + dx) % 4

    def at_peer(r):
        return (z * 4 + ylo * 2 + core, peer_index(r))

    def remote(src, dst, s, r, to):
        return pltpu.make_async_remote_copy(
            src_ref=src, dst_ref=dst, send_sem=s, recv_sem=r,
            device_id=to, device_id_type=MESH)

    barrier = pltpu.get_barrier_semaphore()
    partners = ([at_sub(i) for i in range(1, SUB)] + [at_z(d) for d in DZ[1:]]
                + [at_peer(r) for r in range(1, PEERS)])
    for p in partners:
        pl.semaphore_signal(barrier, inc=1, device_id=p, device_id_type=MESH)

    loads = []
    for r in range(PEERS):
        j = peer_index(r)
        for h in range(2):
            loads.append(pltpu.make_async_copy(
                w_in.at[0, pl.ds(pl.multiple_of(j * 256 + h * 128, 128), 128), :],
                w1.at[h, pl.ds(r * 128, 128), :], w_sem.at[len(loads)]))
        loads.append(pltpu.make_async_copy(
            w_out.at[0, :, pl.ds(pl.multiple_of(j * 256, 256), 256)],
            w2.at[r], w_sem.at[len(loads)]))
    for c in loads:
        c.start()

    e = ids[...]
    dz = (e // 4 - z + NZ) % NZ
    k = jnp.zeros_like(e)
    for d, s in SLOT_OF.items():
        k = jnp.where(dz == d, s, k)
    sub = ((e // 2 % 2 + ylo) % 2) * 2 + (e % 2 + core) % 2
    c = slot[...]
    target = jnp.where(c >= 0, sub * (NZ * CAP) + k * CAP + c, -1)
    rows = lax.broadcasted_iota(jnp.int32, (SUB * NZ * CAP, 256), 0)
    hit0, hit1 = rows == target[0:1, :], rows == target[1:2, :]
    panel = jnp.dot((hit0 | hit1).astype(F32).astype(BF), tok[...], preferred_element_type=F32)
    near_out[...] = panel.astype(BF).reshape(SUB, NZ * CAP, 256)

    pl.semaphore_wait(barrier, len(partners))

    near = []
    for i in range(1, SUB):
        cp = remote(near_out.at[i], near_in.at[i], near_s.at[i], near_r.at[i], at_sub(i))
        cp.start()
        near.append(cp)
    near_in[0] = near_out[0]

    def near_of_far(i, swap):
        kk = (i * 1639) >> 16
        if swap:
            kk = kk + 1 - 2 * (kk % 2)
        rest = i - ((i * 1639) >> 16) * 40
        ss = (rest * 205) >> 11
        return ss * (NZ * CAP) + kk * CAP + rest - ss * 10

    n = SUB * NZ * CAP
    col_i = lax.broadcasted_iota(jnp.int32, (n, n), 1)
    row_i = lax.broadcasted_iota(jnp.int32, (n, n), 0)
    far_rows = lax.broadcasted_iota(jnp.int32, (n, 1), 0)
    far_cols = lax.broadcasted_iota(jnp.int32, (1, n), 1)
    for h in range(2):
        mix[h] = (near_of_far(far_rows, h) == col_i).astype(F32).astype(BF)
        unmix[h] = (near_of_far(far_cols, h) == row_i).astype(F32).astype(BF)

    g = gate[...]
    weighted = jnp.where(hit0, g[0:1, :], 0.0) + jnp.where(hit1, g[1:2, :], 0.0)
    hi = weighted.astype(BF)
    gates_hi[...] = hi.astype(F32).T.astype(BF)
    gates_lo[...] = (weighted - hi.astype(F32)).T.astype(BF)

    upper = lax.broadcasted_iota(jnp.int32, (2 * UNIT, 128), 0) < UNIT

    def pick(a, b):
        return jnp.where(upper, a, b)

    for cp in near:
        cp.wait_recv()

    arrived = near_in[...].reshape(n, 256)
    order0 = jnp.dot(mix[0], arrived[:, :128], preferred_element_type=F32)
    order1 = jnp.dot(mix[1], arrived[:, 128:], preferred_element_type=F32)
    far = []
    for s in range(NZ):
        a = order0[(s // 2) * 80:(s // 2 + 1) * 80]
        b = order1[(s // 2) * 80:(s // 2 + 1) * 80]
        block = (pick(a, b) if s % 2 == 0 else pick(b, a)).astype(BF)
        if s == 0:
            far_in[0, 0] = block
            continue
        far_out[s] = block
        cp = remote(far_out.at[s], far_in.at[0, BACK[s]], far_s.at[s], far_r.at[BACK[s]],
                    at_z(DZ[s]))
        cp.start()
        far.append(cp)

    gathers, scatters, backs = [], [], []

    def gather(g):
        here = pl.ds(g * PER, PER)
        for s in range(g * PER, (g + 1) * PER):
            if s:
                remote(far_out.at[s], far_in.at[0, s], far_s.at[s], far_r.at[s], at_z(DZ[s])).wait_recv()
        for r in range(1, PEERS):
            cp = remote(far_in.at[0, here], far_in.at[OFF_BACK[r], here],
                        ag_s.at[r, g], ag_r.at[OFF_BACK[r], g], at_peer(r))
            cp.start()
            gathers.append(cp)

    def compute(g):
        here = pl.ds(g * PER, PER)
        for r in range(1, PEERS):
            remote(far_in.at[0, here], far_in.at[r, here],
                   ag_s.at[r, g], ag_r.at[r, g], at_peer(r)).wait_recv()
        left0, left1 = [], []
        for q in range(PER // 2):
            s = g * PER + 2 * q
            a0 = [far_in[r, s] for r in range(PEERS)]
            a1 = [far_in[r, s + 1] for r in range(PEERS)]
            left0.append(jnp.concatenate([pick(u, v) for u, v in zip(a0, a1)], axis=1))
            left1.append(jnp.concatenate([pick(v, u) for u, v in zip(a0, a1)], axis=1))
        acc0 = jnp.dot(jnp.concatenate(left0, axis=0), w1[0], preferred_element_type=F32)
        acc1 = jnp.dot(jnp.concatenate(left1, axis=0), w1[1], preferred_element_type=F32)
        swapped = []
        for q in range(PER // 2):
            swapped += [acc1[q * 80 + 40:q * 80 + 80], acc1[q * 80:q * 80 + 40]]
        v = acc0 + jnp.concatenate(swapped, axis=0)
        inner = 0.7978845608028654 * (v + 0.044715 * (v * v * v))
        hidden = (0.5 * v * (1.0 + jnp.tanh(inner))).astype(BF)
        for r in list(range(1, PEERS)) + [0]:
            res = jnp.dot(hidden, w2[r], preferred_element_type=F32)
            for q in range(PER // 2):
                p0 = res[q * 80:q * 80 + 80, :128]
                p1 = res[q * 80:q * 80 + 80, 128:]
                p1 = jnp.concatenate([p1[40:], p1[:40]], axis=0)
                s = g * PER + 2 * q
                part_out[r, s] = pick(p0, p1).astype(BF)
                part_out[r, s + 1] = pick(p1, p0).astype(BF)
            if r:
                cp = remote(part_out.at[r, here], part_in.at[OFF_BACK[r], here],
                            rs_s.at[r, g], rs_r.at[OFF_BACK[r], g], at_peer(r))
                cp.start()
                scatters.append(cp)

    def finish(g):
        here = pl.ds(g * PER, PER)
        for r in range(1, PEERS):
            remote(part_out.at[r, here], part_in.at[r, here],
                   rs_s.at[r, g], rs_r.at[r, g], at_peer(r)).wait_recv()
        for s in range(g * PER, (g + 1) * PER):
            total = part_out[0, s].astype(F32)
            for r in range(1, PEERS):
                total = total + part_in[r, s].astype(F32)
            if s == 0:
                back_in[0] = total.astype(BF)
                continue
            back_out[s] = total.astype(BF)
            cp = remote(back_out.at[s], back_in.at[BACK[s]], back_s.at[s], back_r.at[BACK[s]],
                        at_z(DZ[s]))
            cp.start()
            backs.append(cp)

    gather(0)
    gather(1)
    for cp in loads:
        cp.wait()
    compute(0)
    gather(2)
    compute(1)
    gather(3)
    finish(0)
    compute(2)
    finish(1)
    compute(3)
    finish(2)
    finish(3)

    for s in range(1, NZ):
        remote(back_out.at[s], back_in.at[s], back_s.at[s], back_r.at[s], at_z(DZ[s])).wait_recv()
    left0, left1 = [], []
    for q in range(NZ // 2):
        a, b = back_in[2 * q], back_in[2 * q + 1]
        left0.append(pick(a, b))
        left1.append(pick(b, a))
    res0 = jnp.dot(unmix[0], jnp.concatenate(left0, axis=0), preferred_element_type=F32)
    res1 = jnp.dot(unmix[1], jnp.concatenate(left1, axis=0), preferred_element_type=F32)
    res = jnp.concatenate([res0, res1], axis=1).astype(BF).reshape(SUB, NZ * CAP, 256)
    last = []
    last_out[...] = res
    for i in range(1, SUB):
        cp = remote(last_out.at[i], last_in.at[i], last_s.at[i], last_r.at[i], at_sub(i))
        cp.start()
        last.append(cp)
    last_in[0] = last_out[0]
    for cp in last:
        cp.wait_recv()
    rows_in = last_in[...].reshape(n, 256)
    out[...] = (jnp.dot(gates_hi[...], rows_in, preferred_element_type=F32)
                + jnp.dot(gates_lo[...], rows_in, preferred_element_type=F32)).astype(BF)
    for cp in near + far + gathers + scatters + backs + last:
        cp.wait_send()


def body(tokens, gate_values, expert_ids, slot_index, w_in, w_out):
    n = SUB * NZ * CAP
    vm = pl.BlockSpec(memory_space=pltpu.VMEM)
    hbm = pl.BlockSpec(memory_space=pl.ANY)
    dma = pltpu.SemaphoreType.DMA
    blocks = (NZ, 2 * UNIT, 128)
    return pl.pallas_call(
        kernel,
        out_shape=jax.ShapeDtypeStruct((256, 256), BF),
        in_specs=[vm, vm, vm, vm, hbm, hbm],
        out_specs=vm,
        scratch_shapes=[
            pltpu.VMEM((2, 1024, 512), BF), pltpu.VMEM((PEERS, 512, 256), BF),
            pltpu.VMEM((2, n, n), BF), pltpu.VMEM((2, n, n), BF),
            pltpu.VMEM((256, n), BF), pltpu.VMEM((256, n), BF),
            pltpu.VMEM((SUB, NZ * CAP, 256), BF), pltpu.VMEM((SUB, NZ * CAP, 256), BF),
            pltpu.VMEM(blocks, BF), pltpu.VMEM((PEERS,) + blocks, BF),
            pltpu.VMEM((PEERS,) + blocks, BF), pltpu.VMEM((PEERS,) + blocks, BF),
            pltpu.VMEM(blocks, BF), pltpu.VMEM(blocks, BF),
            pltpu.VMEM((SUB, NZ * CAP, 256), BF), pltpu.VMEM((SUB, NZ * CAP, 256), BF),
            dma((3 * PEERS,)), dma((SUB,)), dma((SUB,)), dma((NZ,)), dma((NZ,)),
            dma((PEERS, GROUPS)), dma((PEERS, GROUPS)), dma((PEERS, GROUPS)), dma((PEERS, GROUPS)),
            dma((NZ,)), dma((NZ,)), dma((SUB,)), dma((SUB,)),
        ],
        compiler_params=pltpu.CompilerParams(
            collective_id=0, has_side_effects=True, vmem_limit_bytes=48 * 2**20),
        name="moe",
    )(tokens, expert_ids.T, slot_index.T, gate_values.T, w_in, w_out)


def solution(mesh):
    placed = (
        P("expert", "tensor"),
        P("expert", None),
        P("expert", None),
        P("expert", None),
        P("expert", None, "tensor"),
        P("expert", "tensor", None),
    )
    return jax.shard_map(
        body, mesh=mesh, in_specs=placed, out_specs=P("expert", "tensor"), check_vma=False
    )
```

```python
import functools

import jax
import jax.numpy as jnp
from jax import lax
from jax.experimental import pallas as pl
from jax.experimental.pallas import tpu as pltpu
from jax.sharding import PartitionSpec as P

MESH = pl.DeviceIdType.MESH
BF, F32 = jnp.bfloat16, jnp.float32

NZ = 16
SUB = 4
CAP = 10
PEERS = 8
UNIT = SUB * CAP
DZ = (1, 2, -1, -2, 3, 4, -3, -4, 5, 6, -5, -6, 0, 7, 8, -7)
SLOT_OF = {d % NZ: k for k, d in enumerate(DZ)}
BACK = tuple(SLOT_OF[(-d) % NZ] for d in DZ)
HALF = NZ * CAP // 2
GROUPS = 4
PER = NZ // GROUPS
ROW = 4
FIRST = {"own": 0, "row": 5, "col": 9, "px": 13, "py": 17, "qx": 21, "qy": 25}


def plan(period, hop, start, wave):
    at = [(-9, "m", 0), (-8, "z", 0), (-7, "m", 1), (-6, "z", 1),
          (wave, "z", 2), (2 * wave, "z", 3), (2 * wave + 0.1, "u", 0), (2 * wave + 0.2, "w", 0)]
    for g in range(GROUPS):
        t = g * period * PER
        at += [(max(t, g * start * PER), "a", g), (t + hop, "b", g), (t + 2 * hop, "d", g),
               (t + 3 * hop, "e", g), (t + 4 * hop, "g", g)]
        if g == GROUPS // 2 - 1:
            at += [(t + 5.5 * hop, "k", 0), (t + 7 * hop, "c", 0)]
    at = sorted(at)
    tail = [("x", i) for i in range(4)] + [("k", 1), ("c", 1)]
    done = [(s, i) for _, s, i in at if (s, i) != ("c", 0)]
    return done + [("c", 0)] + tail


ORDER = plan(1.0, 3.0, 1.0, 0.5)


def places():
    e, t = lax.axis_index("expert"), lax.axis_index("tensor")
    return e // 4, (e // 2) % 2, e % 2, t // 4, t % 4


def kernel(tok_in, ids_in, slot_in, gate_in, w_in, w_out, out,
           tok, ids, slot, gate, in_sem, w1, w2, mix, unmix, gates_hi, gates_lo,
           near_out, near_in, far_out, far_in, part_out, by_x, by_y, last_x, last_y,
           back_out, back_in, last_out, last_in,
           w_sem, near_s, near_r, far_s, far_r, tree_s, tree_r,
           back_s, back_r, last_s, last_r):
    z, ylo, core, yhi, x = places()
    tens = yhi * 4 + x

    def at_sub(i):
        return (z * 4 + ((ylo + i // 2) % 2) * 2 + (core + i % 2) % 2, tens)

    def at_z(d):
        return (((z + d + NZ) % NZ) * 4 + ylo * 2 + core, tens)

    def peer_index(r):
        return ((yhi + r // ROW) % 2) * 4 + (x + r % ROW) % 4

    def at_peer(r):
        return (z * 4 + ylo * 2 + core, peer_index(r))

    def remote(src, dst, s, r, to):
        return pltpu.make_async_remote_copy(
            src_ref=src, dst_ref=dst, send_sem=s, recv_sem=r,
            device_id=to, device_id_type=MESH)

    barrier = pltpu.get_barrier_semaphore()
    partners = ([at_sub(i) for i in range(1, SUB)] + [at_z(d) for d in range(1, NZ)]
                + [at_peer(r) for r in (1, 2, 3, ROW)])
    for p in partners:
        pl.semaphore_signal(barrier, inc=1, device_id=p, device_id_type=MESH)

    firsts = [pltpu.make_async_copy(a, b, in_sem.at[i]) for i, (a, b) in enumerate(
        ((ids_in, ids), (slot_in, slot), (tok_in, tok), (gate_in, gate)))]
    for cp in firsts:
        cp.start()
    loads = []
    for r in range(PEERS):
        j = peer_index(r)
        for h in range(2):
            loads.append(pltpu.make_async_copy(
                w_in.at[0, pl.ds(pl.multiple_of(j * 256 + h * 128, 128), 128), :],
                w1.at[h, pl.ds(r * 128, 128), :], w_sem.at[len(loads)]))
        loads.append(pltpu.make_async_copy(
            w_out.at[0, :, pl.ds(pl.multiple_of(j * 256, 256), 256)],
            w2.at[r], w_sem.at[len(loads)]))
    for c in loads:
        c.start()

    for cp in firsts:
        cp.wait()
    e = ids[...]
    dz = (e // 4 - z + NZ) % NZ
    k = jnp.zeros_like(e)
    for d, s in SLOT_OF.items():
        k = jnp.where(dz == d, s, k)
    sub = ((e // 2 % 2 + ylo) % 2) * 2 + (e % 2 + core) % 2
    c = slot[...]
    half_k = k // (NZ // 2)
    target = jnp.where(c >= 0, (half_k * SUB + sub - half_k) * HALF + k * CAP + c, -1)
    rows = lax.broadcasted_iota(jnp.int32, (SUB * NZ * CAP, 256), 0)
    chosen = (rows == target[0:1, :]) | (rows == target[1:2, :])
    panel = jnp.dot(chosen.astype(F32).astype(BF), tok[...], preferred_element_type=F32)
    near_out[...] = panel.astype(BF).reshape(2, SUB, HALF, 256)

    pl.semaphore_wait(barrier, len(partners))

    near = []
    for half in range(2):
        for i in range(1, SUB):
            cp = remote(near_out.at[half, i], near_in.at[half, i], near_s.at[half, i],
                        near_r.at[half, i], at_sub(i))
            cp.start()
            near.append(cp)
    near_in[:, 0] = near_out[:, 0]

    def near_of_far(i, swap):
        kk = (i * 1639) >> 16
        rest = i - kk * 40
        if swap:
            kk = kk + 1 - 2 * (kk % 2)
        ss = (rest * 205) >> 11
        return ss * HALF + kk * CAP + rest - ss * 10

    n = SUB * HALF
    near_cols = lax.broadcasted_iota(jnp.int32, (n, n), 1)
    near_rows = lax.broadcasted_iota(jnp.int32, (n, n), 0)
    far_rows = lax.broadcasted_iota(jnp.int32, (n, 1), 0)
    far_cols = lax.broadcasted_iota(jnp.int32, (1, n), 1)
    for h in range(2):
        mix[h] = (near_of_far(far_rows, h) == near_cols).astype(F32).astype(BF)

    upper = lax.broadcasted_iota(jnp.int32, (2 * UNIT, 128), 0) < UNIT

    def pick(a, b):
        return jnp.where(upper, a, b)

    far = {}

    def arrange(half):
        for cp in near[half * 3:half * 3 + 3]:
            cp.wait_recv()
        arrived = near_in[half].reshape(n, 256)
        order0 = jnp.dot(mix[0], arrived[:, :128], preferred_element_type=F32)
        order1 = jnp.dot(mix[1], arrived[:, 128:], preferred_element_type=F32)
        for k in range(NZ // 2):
            s = half * (NZ // 2) + k
            a = order0[(k // 2) * 80:(k // 2 + 1) * 80]
            b = order1[(k // 2) * 80:(k // 2 + 1) * 80]
            block = (pick(a, b) if s % 2 == 0 else pick(b, a)).astype(BF)
            if DZ[s] == 0:
                far_in[0, s] = block
            else:
                far_out[s] = block

    def spread(g):
        for s in range(g * 4, g * 4 + 4):
            if DZ[s]:
                far[s] = remote(far_out.at[s], far_in.at[0, BACK[s]], far_s.at[s],
                                far_r.at[BACK[s]], at_z(DZ[s]))
                far[s].start()

    def drain(g):
        for s in range(g * 4, g * 4 + 4):
            if DZ[s]:
                far[s].wait_send()

    def prepare(_):
        for h in range(2):
            unmix[h] = (near_of_far(far_cols, h) == near_rows).astype(F32).astype(BF)
        g = gate[...]
        weighted = jnp.where(rows == target[0:1, :], g[0:1, :], 0.0) + jnp.where(
            rows == target[1:2, :], g[1:2, :], 0.0)
        hi = weighted.astype(BF)
        lo = weighted - hi.astype(F32)
        for half in range(2):
            gates_hi[half] = hi[half * n:(half + 1) * n].astype(F32).T.astype(BF)
            gates_lo[half] = lo[half * n:(half + 1) * n].T.astype(BF)

    def loaded(_):
        for cp in loads:
            cp.wait()

    sent = {}
    backs = []
    H = PER // 2

    def send(g, kind, i, src, dst, to):
        n = FIRST[kind] + i
        cp = remote(src, dst, tree_s.at[g, n], tree_r.at[g, n], at_peer(to))
        cp.start()
        sent[g, kind, i] = cp

    def got(g, kind, *which):
        for i in which:
            sent[g, kind, i].wait_recv()

    def part(g, half):
        return pl.ds(g * PER + half * H, H)

    def gather0(g):
        for s in range(g * PER, (g + 1) * PER):
            if DZ[s]:
                remote(far_out.at[s], far_in.at[0, s], far_s.at[s], far_r.at[s], at_z(DZ[s])).wait_recv()
        whole = pl.ds(g * PER, PER)
        for r in (ROW, 1, 3, 2):
            back = r if r == ROW else 4 - r
            send(g, "own", back, far_in.at[0, whole], far_in.at[back, whole], r)

    def gather1(g):
        got(g, "own", ROW)
        for r in (1, 3, 2):
            send(g, "row", 4 - r, far_in.at[ROW, part(g, 0)], far_in.at[ROW + 4 - r, part(g, 0)], r)
        for r in (1, 3, 2):
            got(g, "own", r)
            send(g, "col", r, far_in.at[r, part(g, 1)], far_in.at[ROW + r, part(g, 1)], ROW)

    def compute(g):
        got(g, "row", 1, 2, 3)
        got(g, "col", 1, 2, 3)
        left0, left1 = [], []
        for q in range(H):
            s = g * PER + 2 * q
            a0 = [far_in[r, s] for r in range(PEERS)]
            a1 = [far_in[r, s + 1] for r in range(PEERS)]
            left0.append(jnp.concatenate([pick(u, v) for u, v in zip(a0, a1)], axis=1))
            left1.append(jnp.concatenate([pick(v, u) for u, v in zip(a0, a1)], axis=1))
        acc0 = jnp.dot(jnp.concatenate(left0, axis=0), w1[0], preferred_element_type=F32)
        acc1 = jnp.dot(jnp.concatenate(left1, axis=0), w1[1], preferred_element_type=F32)
        swapped = []
        for q in range(H):
            swapped += [acc1[q * 80 + 40:q * 80 + 80], acc1[q * 80:q * 80 + 40]]
        v = acc0 + jnp.concatenate(swapped, axis=0)
        inner = 0.7978845608028654 * (v + 0.044715 * (v * v * v))
        hidden = (0.5 * v * (1.0 + jnp.tanh(inner))).astype(BF)
        for r in (5, 1, 7, 3, 6, 2, 4, 0):
            res = jnp.dot(hidden, w2[r], preferred_element_type=F32)
            for q in range(H):
                p0 = res[q * 80:q * 80 + 80, :128]
                p1 = res[q * 80:q * 80 + 80, 128:]
                p1 = jnp.concatenate([p1[40:], p1[:40]], axis=0)
                s = g * PER + 2 * q
                part_out[r // 4, r % 4, s] = pick(p0, p1).astype(BF)
                part_out[r // 4, r % 4, s + 1] = pick(p1, p0).astype(BF)
            if r in (1, 2, 3):
                send(g, "px", 4 - r, part_out.at[:, r, part(g, 0)], by_x.at[g, 4 - r], r)
            if r >= ROW:
                send(g, "py", r - ROW, part_out.at[1, r - ROW, part(g, 1)], by_y.at[g, r - ROW], ROW)

    def scatter1(g):
        for r in (1, 3, 2):
            got(g, "py", r)
            for i in range(H):
                s = g * PER + H + i
                part_out[0, r, s] = (part_out[0, r, s].astype(F32) + by_y[g, r, i].astype(F32)).astype(BF)
            send(g, "qx", 4 - r, part_out.at[0, r, part(g, 1)], last_x.at[g, 4 - r], r)
        got(g, "px", 1, 2, 3)
        for i in range(H):
            s = g * PER + i
            total = part_out[1, 0, s].astype(F32)
            for r in (1, 2, 3):
                total = total + by_x[g, r, 1, i].astype(F32)
            part_out[1, 0, s] = total.astype(BF)
        send(g, "qy", 0, part_out.at[1, 0, part(g, 0)], last_y.at[g], ROW)

    def give_back(s, value):
        if DZ[s] == 0:
            back_in[s] = value.astype(BF)
            return
        back_out[s] = value.astype(BF)
        cp = remote(back_out.at[s], back_in.at[BACK[s]], back_s.at[s], back_r.at[BACK[s]],
                    at_z(DZ[s]))
        cp.start()
        backs.append(cp)

    def finish(g):
        got(g, "qy", 0)
        for i in range(H):
            s = g * PER + i
            total = part_out[0, 0, s].astype(F32) + last_y[g, i].astype(F32)
            for r in (1, 2, 3):
                total = total + by_x[g, r, 0, i].astype(F32)
            give_back(s, total)
        got(g, "py", 0)
        got(g, "qx", 1, 2, 3)
        for i in range(H):
            s = g * PER + H + i
            total = part_out[0, 0, s].astype(F32) + by_y[g, 0, i].astype(F32)
            for r in (1, 2, 3):
                total = total + last_x[g, r, i].astype(F32)
            give_back(s, total)

    last = []

    def returned(half):
        for s in range(half * NZ // 2, (half + 1) * NZ // 2):
            if DZ[s]:
                remote(back_out.at[s], back_in.at[s], back_s.at[s], back_r.at[s],
                       at_z(DZ[s])).wait_recv()
        left0, left1 = [], []
        for q in range(half * NZ // 4, (half + 1) * NZ // 4):
            a, b = back_in[2 * q], back_in[2 * q + 1]
            left0.append(pick(a, b))
            left1.append(pick(b, a))
        res0 = jnp.dot(unmix[0], jnp.concatenate(left0, axis=0), preferred_element_type=F32)
        res1 = jnp.dot(unmix[1], jnp.concatenate(left1, axis=0), preferred_element_type=F32)
        res = jnp.concatenate([res0, res1], axis=1).astype(BF)
        last_in[half, 0] = res[:HALF]
        for i in range(1, SUB):
            last_out[half, i] = res[i * HALF:(i + 1) * HALF]
            cp = remote(last_out.at[half, i], last_in.at[half, i], last_s.at[half, i],
                        last_r.at[half, i], at_sub(i))
            cp.start()
            last.append(cp)

    sums = []

    def combine(half):
        for cp in last[half * 3:half * 3 + 3]:
            cp.wait_recv()
        rows_in = last_in[half].reshape(n, 256)
        sums.append(jnp.dot(gates_hi[half], rows_in, preferred_element_type=F32)
                    + jnp.dot(gates_lo[half], rows_in, preferred_element_type=F32))

    steps = {"m": arrange, "z": spread, "x": drain, "u": prepare, "w": loaded,
             "a": gather0, "b": gather1, "d": compute, "e": scatter1, "g": finish,
             "k": returned, "c": combine}
    for step, i in ORDER:
        steps[step](i)
    out[...] = (sums[0] + sums[1]).astype(BF)
    for cp in near + list(sent.values()) + backs + last:
        cp.wait_send()


def body(tokens, gate_values, expert_ids, slot_index, w_in, w_out):
    n = SUB * NZ * CAP
    vm = pl.BlockSpec(memory_space=pltpu.VMEM)
    hbm = pl.BlockSpec(memory_space=pl.ANY)
    dma = pltpu.SemaphoreType.DMA
    blocks = (NZ, 2 * UNIT, 128)
    return pl.pallas_call(
        kernel,
        out_shape=jax.ShapeDtypeStruct((256, 256), BF),
        in_specs=[hbm] * 6,
        out_specs=vm,
        scratch_shapes=[
            pltpu.VMEM((256, 256), BF), pltpu.VMEM((2, 256), jnp.int32),
            pltpu.VMEM((2, 256), jnp.int32), pltpu.VMEM((2, 256), F32), dma((4,)),
            pltpu.VMEM((2, 1024, 512), BF), pltpu.VMEM((PEERS, 512, 256), BF),
            pltpu.VMEM((2, n // 2, n // 2), BF), pltpu.VMEM((2, n // 2, n // 2), BF),
            pltpu.VMEM((2, 256, n // 2), BF), pltpu.VMEM((2, 256, n // 2), BF),
            pltpu.VMEM((2, SUB, HALF, 256), BF), pltpu.VMEM((2, SUB, HALF, 256), BF),
            pltpu.VMEM(blocks, BF), pltpu.VMEM((PEERS,) + blocks, BF),
            pltpu.VMEM((2, 4) + blocks, BF),
            pltpu.VMEM((GROUPS, 4, 2, PER // 2) + blocks[1:], BF),
            pltpu.VMEM((GROUPS, 4, PER // 2) + blocks[1:], BF),
            pltpu.VMEM((GROUPS, 4, PER // 2) + blocks[1:], BF),
            pltpu.VMEM((GROUPS, PER // 2) + blocks[1:], BF),
            pltpu.VMEM(blocks, BF), pltpu.VMEM(blocks, BF),
            pltpu.VMEM((2, SUB, HALF, 256), BF), pltpu.VMEM((2, SUB, HALF, 256), BF),
            dma((3 * PEERS,)), dma((2, SUB)), dma((2, SUB)), dma((NZ,)), dma((NZ,)),
            dma((GROUPS, 26)), dma((GROUPS, 26)),
            dma((NZ,)), dma((NZ,)), dma((2, SUB)), dma((2, SUB)),
        ],
        compiler_params=pltpu.CompilerParams(
            collective_id=0, has_side_effects=True, vmem_limit_bytes=60 * 2**20),
        name="moe",
    )(tokens, expert_ids.T, slot_index.T, gate_values.T, w_in, w_out)


def solution(mesh):
    placed = (
        P("expert", "tensor"),
        P("expert", None),
        P("expert", None),
        P("expert", None),
        P("expert", None, "tensor"),
        P("expert", "tensor", None),
    )
    return jax.shard_map(
        body, mesh=mesh, in_specs=placed, out_specs=P("expert", "tensor"), check_vma=False
    )
```

```python
import functools

import jax
import jax.numpy as jnp
from jax import lax
from jax.experimental import pallas as pl
from jax.experimental.pallas import tpu as pltpu
from jax.sharding import PartitionSpec as P

MESH = pl.DeviceIdType.MESH
BF, F32 = jnp.bfloat16, jnp.float32

NZ = 16
SUB = 4
CAP = 10
PEERS = 8
UNIT = SUB * CAP
DZ = (1, 2, -1, -2, 3, 4, -3, -4, 0, 7, 8, -7, 5, 6, -5, -6)
SLOT_OF = {d % NZ: k for k, d in enumerate(DZ)}
BACK = tuple(SLOT_OF[(-d) % NZ] for d in DZ)
HALF = NZ * CAP // 2
GROUPS = 4
PER = NZ // GROUPS
ROW = 4
FIRST = {"own": 0, "row": 5, "col": 9, "px": 13, "py": 17, "qx": 21, "qy": 25}


def plan(period, hop, start, wave):
    at = [(-9, "m", 0), (-8, "z", 0), (-7, "m", 1), (-6, "z", 1),
          (wave, "z", 2), (2 * wave, "z", 3), (2 * wave + 0.1, "u", 0), (2 * wave + 0.2, "w", 0)]
    for g in range(GROUPS):
        t = g * period * PER
        at += [(max(t, g * start * PER), "a", g), (t + hop, "b", g), (t + 2 * hop, "d", g),
               (t + 3 * hop, "e", g), (t + 4 * hop, "g", g)]
        if g == GROUPS // 2 - 1:
            at += [(t + 5.5 * hop, "k", 0), (t + 7 * hop, "c", 0)]
    at = sorted(at)
    tail = [("x", i) for i in range(4)] + [("k", 1), ("c", 1)]
    done = [(s, i) for _, s, i in at if (s, i) != ("c", 0)]
    return done + [("c", 0)] + tail


ORDER = plan(1.0, 3.0, 1.0, 0.5)


def places():
    e, t = lax.axis_index("expert"), lax.axis_index("tensor")
    return e // 4, (e // 2) % 2, e % 2, t // 4, t % 4


def kernel(tok_in, ids_in, slot_in, gate_in, w_in, w_out, out,
           tok, ids, slot, gate, in_sem, w1, w2, mix, unmix, gates_hi, gates_lo,
           near_out, near_in, far_out, far_in, part_out, by_x, by_y, last_x, last_y,
           back_out, back_in, last_out, last_in,
           w_sem, near_s, near_r, far_s, far_r, tree_s, tree_r,
           back_s, back_r, last_s, last_r):
    z, ylo, core, yhi, x = places()
    tens = yhi * 4 + x

    def at_sub(i):
        return (z * 4 + ((ylo + i // 2) % 2) * 2 + (core + i % 2) % 2, tens)

    def at_z(d):
        return (((z + d + NZ) % NZ) * 4 + ylo * 2 + core, tens)

    def peer_index(r):
        return ((yhi + r // ROW) % 2) * 4 + (x + r % ROW) % 4

    def at_peer(r):
        return (z * 4 + ylo * 2 + core, peer_index(r))

    def remote(src, dst, s, r, to):
        return pltpu.make_async_remote_copy(
            src_ref=src, dst_ref=dst, send_sem=s, recv_sem=r,
            device_id=to, device_id_type=MESH)

    barrier = pltpu.get_barrier_semaphore()
    partners = ([at_sub(i) for i in range(1, SUB)] + [at_z(d) for d in range(1, NZ)]
                + [at_peer(r) for r in (1, 2, 3, ROW)])
    for p in partners:
        pl.semaphore_signal(barrier, inc=1, device_id=p, device_id_type=MESH)

    firsts = [pltpu.make_async_copy(a, b, in_sem.at[i]) for i, (a, b) in enumerate(
        ((ids_in, ids), (slot_in, slot), (tok_in, tok), (gate_in, gate)))]
    for cp in firsts:
        cp.start()
    loads = []
    for r in range(PEERS):
        j = peer_index(r)
        for h in range(2):
            loads.append(pltpu.make_async_copy(
                w_in.at[0, pl.ds(pl.multiple_of(j * 256 + h * 128, 128), 128), :],
                w1.at[h, pl.ds(r * 128, 128), :], w_sem.at[len(loads)]))
        loads.append(pltpu.make_async_copy(
            w_out.at[0, :, pl.ds(pl.multiple_of(j * 256, 256), 256)],
            w2.at[r], w_sem.at[len(loads)]))
    for c in loads:
        c.start()

    for cp in firsts:
        cp.wait()
    e = ids[...]
    dz = (e // 4 - z + NZ) % NZ
    k = jnp.zeros_like(e)
    for d, s in SLOT_OF.items():
        k = jnp.where(dz == d, s, k)
    sub = ((e // 2 % 2 + ylo) % 2) * 2 + (e % 2 + core) % 2
    c = slot[...]
    half_k = k // (NZ // 2)
    target = jnp.where(c >= 0, (half_k * SUB + sub - half_k) * HALF + k * CAP + c, -1)
    rows = lax.broadcasted_iota(jnp.int32, (SUB * NZ * CAP, 256), 0)
    chosen = (rows == target[0:1, :]) | (rows == target[1:2, :])
    panel = jnp.dot(chosen.astype(F32).astype(BF), tok[...], preferred_element_type=F32)
    near_out[...] = panel.astype(BF).reshape(2, SUB, HALF, 256)

    pl.semaphore_wait(barrier, len(partners))

    near = []
    for half in range(2):
        for i in range(1, SUB):
            cp = remote(near_out.at[half, i], near_in.at[half, i], near_s.at[half, i],
                        near_r.at[half, i], at_sub(i))
            cp.start()
            near.append(cp)
    near_in[:, 0] = near_out[:, 0]

    def near_of_far(i, swap):
        kk = (i * 1639) >> 16
        rest = i - kk * 40
        if swap:
            kk = kk + 1 - 2 * (kk % 2)
        ss = (rest * 205) >> 11
        return ss * HALF + kk * CAP + rest - ss * 10

    n = SUB * HALF
    near_cols = lax.broadcasted_iota(jnp.int32, (n, n), 1)
    near_rows = lax.broadcasted_iota(jnp.int32, (n, n), 0)
    far_rows = lax.broadcasted_iota(jnp.int32, (n, 1), 0)
    far_cols = lax.broadcasted_iota(jnp.int32, (1, n), 1)
    for h in range(2):
        mix[h] = (near_of_far(far_rows, h) == near_cols).astype(F32).astype(BF)

    upper = lax.broadcasted_iota(jnp.int32, (2 * UNIT, 128), 0) < UNIT

    def pick(a, b):
        return jnp.where(upper, a, b)

    far = {}

    def arrange(half):
        for cp in near[half * 3:half * 3 + 3]:
            cp.wait_recv()
        arrived = near_in[half].reshape(n, 256)
        order0 = jnp.dot(mix[0], arrived[:, :128], preferred_element_type=F32)
        order1 = jnp.dot(mix[1], arrived[:, 128:], preferred_element_type=F32)
        for k in range(NZ // 2):
            s = half * (NZ // 2) + k
            a = order0[(k // 2) * 80:(k // 2 + 1) * 80]
            b = order1[(k // 2) * 80:(k // 2 + 1) * 80]
            block = (pick(a, b) if s % 2 == 0 else pick(b, a)).astype(BF)
            if DZ[s] == 0:
                far_in[0, s] = block
            else:
                far_out[s] = block

    def spread(g):
        for s in range(g * 4, g * 4 + 4):
            if DZ[s]:
                far[s] = remote(far_out.at[s], far_in.at[0, BACK[s]], far_s.at[s],
                                far_r.at[BACK[s]], at_z(DZ[s]))
                far[s].start()

    def drain(g):
        for s in range(g * 4, g * 4 + 4):
            if DZ[s]:
                far[s].wait_send()

    def prepare(_):
        for h in range(2):
            unmix[h] = (near_of_far(far_cols, h) == near_rows).astype(F32).astype(BF)
        g = gate[...]
        weighted = jnp.where(rows == target[0:1, :], g[0:1, :], 0.0) + jnp.where(
            rows == target[1:2, :], g[1:2, :], 0.0)
        hi = weighted.astype(BF)
        lo = weighted - hi.astype(F32)
        for half in range(2):
            gates_hi[half] = hi[half * n:(half + 1) * n].astype(F32).T.astype(BF)
            gates_lo[half] = lo[half * n:(half + 1) * n].T.astype(BF)

    def loaded(_):
        for cp in loads:
            cp.wait()

    sent = {}
    backs = []
    H = PER // 2

    def send(g, kind, i, src, dst, to):
        n = FIRST[kind] + i
        cp = remote(src, dst, tree_s.at[g, n], tree_r.at[g, n], at_peer(to))
        cp.start()
        sent[g, kind, i] = cp

    def got(g, kind, *which):
        for i in which:
            sent[g, kind, i].wait_recv()

    def part(g, half):
        return pl.ds(g * PER + half * H, H)

    def gather0(g):
        for s in range(g * PER, (g + 1) * PER):
            if DZ[s]:
                remote(far_out.at[s], far_in.at[0, s], far_s.at[s], far_r.at[s], at_z(DZ[s])).wait_recv()
        whole = pl.ds(g * PER, PER)
        for r in (ROW, 1, 3, 2):
            back = r if r == ROW else 4 - r
            send(g, "own", back, far_in.at[0, whole], far_in.at[back, whole], r)

    def gather1(g):
        got(g, "own", ROW)
        for r in (1, 3, 2):
            send(g, "row", 4 - r, far_in.at[ROW, part(g, 0)], far_in.at[ROW + 4 - r, part(g, 0)], r)
        for r in (1, 3, 2):
            got(g, "own", r)
            send(g, "col", r, far_in.at[r, part(g, 1)], far_in.at[ROW + r, part(g, 1)], ROW)

    def compute(g):
        got(g, "row", 1, 2, 3)
        got(g, "col", 1, 2, 3)
        left0, left1 = [], []
        for q in range(H):
            s = g * PER + 2 * q
            a0 = [far_in[r, s] for r in range(PEERS)]
            a1 = [far_in[r, s + 1] for r in range(PEERS)]
            left0.append(jnp.concatenate([pick(u, v) for u, v in zip(a0, a1)], axis=1))
            left1.append(jnp.concatenate([pick(v, u) for u, v in zip(a0, a1)], axis=1))
        acc0 = jnp.dot(jnp.concatenate(left0, axis=0), w1[0], preferred_element_type=F32)
        acc1 = jnp.dot(jnp.concatenate(left1, axis=0), w1[1], preferred_element_type=F32)
        swapped = []
        for q in range(H):
            swapped += [acc1[q * 80 + 40:q * 80 + 80], acc1[q * 80:q * 80 + 40]]
        v = acc0 + jnp.concatenate(swapped, axis=0)
        inner = 0.7978845608028654 * (v + 0.044715 * (v * v * v))
        hidden = (0.5 * v * (1.0 + jnp.tanh(inner))).astype(BF)
        for r in (5, 7, 6, 1, 3, 2, 4, 0):
            res = jnp.dot(hidden, w2[r], preferred_element_type=F32)
            for q in range(H):
                p0 = res[q * 80:q * 80 + 80, :128]
                p1 = res[q * 80:q * 80 + 80, 128:]
                p1 = jnp.concatenate([p1[40:], p1[:40]], axis=0)
                s = g * PER + 2 * q
                part_out[r // 4, r % 4, s] = pick(p0, p1).astype(BF)
                part_out[r // 4, r % 4, s + 1] = pick(p1, p0).astype(BF)
            if r in (1, 2, 3):
                send(g, "px", 4 - r, part_out.at[:, r, part(g, 0)], by_x.at[g, 4 - r], r)
            if r >= ROW:
                send(g, "py", r - ROW, part_out.at[1, r - ROW, part(g, 1)], by_y.at[g, r - ROW], ROW)

    def scatter1(g):
        for r in (1, 3, 2):
            got(g, "py", r)
            for i in range(H):
                s = g * PER + H + i
                part_out[0, r, s] = (part_out[0, r, s].astype(F32) + by_y[g, r, i].astype(F32)).astype(BF)
            send(g, "qx", 4 - r, part_out.at[0, r, part(g, 1)], last_x.at[g, 4 - r], r)
        got(g, "px", 1, 2, 3)
        for i in range(H):
            s = g * PER + i
            total = part_out[1, 0, s].astype(F32)
            for r in (1, 2, 3):
                total = total + by_x[g, r, 1, i].astype(F32)
            part_out[1, 0, s] = total.astype(BF)
        send(g, "qy", 0, part_out.at[1, 0, part(g, 0)], last_y.at[g], ROW)

    def give_back(s, value):
        if DZ[s] == 0:
            back_in[s] = value.astype(BF)
            return
        back_out[s] = value.astype(BF)
        cp = remote(back_out.at[s], back_in.at[BACK[s]], back_s.at[s], back_r.at[BACK[s]],
                    at_z(DZ[s]))
        cp.start()
        backs.append(cp)

    def finish(g):
        got(g, "qy", 0)
        for i in range(H):
            s = g * PER + i
            total = part_out[0, 0, s].astype(F32) + last_y[g, i].astype(F32)
            for r in (1, 2, 3):
                total = total + by_x[g, r, 0, i].astype(F32)
            give_back(s, total)
        got(g, "py", 0)
        got(g, "qx", 1, 2, 3)
        for i in range(H):
            s = g * PER + H + i
            total = part_out[0, 0, s].astype(F32) + by_y[g, 0, i].astype(F32)
            for r in (1, 2, 3):
                total = total + last_x[g, r, i].astype(F32)
            give_back(s, total)

    last = []

    def returned(half):
        for s in range(half * NZ // 2, (half + 1) * NZ // 2):
            if DZ[s]:
                remote(back_out.at[s], back_in.at[s], back_s.at[s], back_r.at[s],
                       at_z(DZ[s])).wait_recv()
        left0, left1 = [], []
        for q in range(half * NZ // 4, (half + 1) * NZ // 4):
            a, b = back_in[2 * q], back_in[2 * q + 1]
            left0.append(pick(a, b))
            left1.append(pick(b, a))
        res0 = jnp.dot(unmix[0], jnp.concatenate(left0, axis=0), preferred_element_type=F32)
        res1 = jnp.dot(unmix[1], jnp.concatenate(left1, axis=0), preferred_element_type=F32)
        res = jnp.concatenate([res0, res1], axis=1).astype(BF)
        last_in[half, 0] = res[:HALF]
        for i in range(1, SUB):
            last_out[half, i] = res[i * HALF:(i + 1) * HALF]
            cp = remote(last_out.at[half, i], last_in.at[half, i], last_s.at[half, i],
                        last_r.at[half, i], at_sub(i))
            cp.start()
            last.append(cp)

    sums = []

    def combine(half):
        for cp in last[half * 3:half * 3 + 3]:
            cp.wait_recv()
        rows_in = last_in[half].reshape(n, 256)
        sums.append(jnp.dot(gates_hi[half], rows_in, preferred_element_type=F32)
                    + jnp.dot(gates_lo[half], rows_in, preferred_element_type=F32))

    steps = {"m": arrange, "z": spread, "x": drain, "u": prepare, "w": loaded,
             "a": gather0, "b": gather1, "d": compute, "e": scatter1, "g": finish,
             "k": returned, "c": combine}
    for step, i in ORDER:
        steps[step](i)
    out[...] = (sums[0] + sums[1]).astype(BF)
    for cp in near + list(sent.values()) + backs + last:
        cp.wait_send()


def body(tokens, gate_values, expert_ids, slot_index, w_in, w_out):
    n = SUB * NZ * CAP
    vm = pl.BlockSpec(memory_space=pltpu.VMEM)
    hbm = pl.BlockSpec(memory_space=pl.ANY)
    dma = pltpu.SemaphoreType.DMA
    blocks = (NZ, 2 * UNIT, 128)
    return pl.pallas_call(
        kernel,
        out_shape=jax.ShapeDtypeStruct((256, 256), BF),
        in_specs=[hbm] * 6,
        out_specs=vm,
        scratch_shapes=[
            pltpu.VMEM((256, 256), BF), pltpu.VMEM((2, 256), jnp.int32),
            pltpu.VMEM((2, 256), jnp.int32), pltpu.VMEM((2, 256), F32), dma((4,)),
            pltpu.VMEM((2, 1024, 512), BF), pltpu.VMEM((PEERS, 512, 256), BF),
            pltpu.VMEM((2, n // 2, n // 2), BF), pltpu.VMEM((2, n // 2, n // 2), BF),
            pltpu.VMEM((2, 256, n // 2), BF), pltpu.VMEM((2, 256, n // 2), BF),
            pltpu.VMEM((2, SUB, HALF, 256), BF), pltpu.VMEM((2, SUB, HALF, 256), BF),
            pltpu.VMEM(blocks, BF), pltpu.VMEM((PEERS,) + blocks, BF),
            pltpu.VMEM((2, 4) + blocks, BF),
            pltpu.VMEM((GROUPS, 4, 2, PER // 2) + blocks[1:], BF),
            pltpu.VMEM((GROUPS, 4, PER // 2) + blocks[1:], BF),
            pltpu.VMEM((GROUPS, 4, PER // 2) + blocks[1:], BF),
            pltpu.VMEM((GROUPS, PER // 2) + blocks[1:], BF),
            pltpu.VMEM(blocks, BF), pltpu.VMEM(blocks, BF),
            pltpu.VMEM((2, SUB, HALF, 256), BF), pltpu.VMEM((2, SUB, HALF, 256), BF),
            dma((3 * PEERS,)), dma((2, SUB)), dma((2, SUB)), dma((NZ,)), dma((NZ,)),
            dma((GROUPS, 26)), dma((GROUPS, 26)),
            dma((NZ,)), dma((NZ,)), dma((2, SUB)), dma((2, SUB)),
        ],
        compiler_params=pltpu.CompilerParams(
            collective_id=0, has_side_effects=True, vmem_limit_bytes=60 * 2**20),
        name="moe",
    )(tokens, expert_ids.T, slot_index.T, gate_values.T, w_in, w_out)


def solution(mesh):
    placed = (
        P("expert", "tensor"),
        P("expert", None),
        P("expert", None),
        P("expert", None),
        P("expert", None, "tensor"),
        P("expert", "tensor", None),
    )
    return jax.shard_map(
        body, mesh=mesh, in_specs=placed, out_specs=P("expert", "tensor"), check_vma=False
    )
```

```python
import functools

import jax
import jax.numpy as jnp
from jax import lax
from jax.experimental import pallas as pl
from jax.experimental.pallas import tpu as pltpu
from jax.sharding import PartitionSpec as P

MESH = pl.DeviceIdType.MESH
BF, F32 = jnp.bfloat16, jnp.float32

NZ = 16
SUB = 4
CAP = 10
PEERS = 8
UNIT = SUB * CAP
DZ = (1, 2, -1, -2, 3, 4, -3, -4, 0, 7, 8, -7, 5, 6, -5, -6)
SLOT_OF = {d % NZ: k for k, d in enumerate(DZ)}
BACK = tuple(SLOT_OF[(-d) % NZ] for d in DZ)
HALF = NZ * CAP // 2
GROUPS = 4
PER = NZ // GROUPS
ROW = 4
FIRST = {"own": 0, "row": 5, "col": 9, "px": 13, "py": 17, "qx": 21, "qy": 25, "rest": 26}


def plan(period, hop, start, wave):
    at = [(-9, "m", 0), (-8, "z", 0), (-7, "m", 1), (-6, "z", 1),
          (wave, "z", 2), (2 * wave, "z", 3), (2 * wave + 0.1, "u", 0), (2 * wave + 0.2, "w", 0)]
    for g in range(GROUPS):
        t = g * period * PER
        at += [(max(t, g * start * PER), "a", g), (t + hop, "b", g), (t + 2 * hop, "d", g),
               (t + 3 * hop, "e", g), (t + 4 * hop, "g", g)]
        if g == GROUPS // 2 - 1:
            at += [(t + 6 * hop, "k", 0), (t + 7 * hop, "c", 0)]
    at = sorted(at)
    tail = [("x", i) for i in range(4)] + [("k", 1), ("c", 1)]
    done = [(s, i) for _, s, i in at if (s, i) != ("c", 0)]
    return done + [("c", 0)] + tail


ORDER = plan(1.0, 3.0, 1.0, 0.5)


def places():
    e, t = lax.axis_index("expert"), lax.axis_index("tensor")
    return e // 4, (e // 2) % 2, e % 2, t // 4, t % 4


def kernel(tok_in, ids_in, slot_in, gate_in, w_in, w_out, out,
           tok, ids, slot, gate, in_sem, w1, w2, mix, unmix, gates_hi, gates_lo,
           near_out, near_in, far_out, far_in, part_out, by_x, by_y, last_x, last_y,
           back_out, back_in, last_out, last_in,
           w_sem, near_s, near_r, far_s, far_r, tree_s, tree_r,
           back_s, back_r, last_s, last_r):
    z, ylo, core, yhi, x = places()
    tens = yhi * 4 + x

    def at_sub(i):
        return (z * 4 + ((ylo + i // 2) % 2) * 2 + (core + i % 2) % 2, tens)

    def at_z(d):
        return (((z + d + NZ) % NZ) * 4 + ylo * 2 + core, tens)

    def peer_index(r):
        return ((yhi + r // ROW) % 2) * 4 + (x + r % ROW) % 4

    def at_peer(r):
        return (z * 4 + ylo * 2 + core, peer_index(r))

    def remote(src, dst, s, r, to):
        return pltpu.make_async_remote_copy(
            src_ref=src, dst_ref=dst, send_sem=s, recv_sem=r,
            device_id=to, device_id_type=MESH)

    barrier = pltpu.get_barrier_semaphore()
    partners = ([at_sub(i) for i in range(1, SUB)] + [at_z(d) for d in range(1, NZ)]
                + [at_peer(r) for r in (1, 2, 3, ROW)])
    for p in partners:
        pl.semaphore_signal(barrier, inc=1, device_id=p, device_id_type=MESH)

    firsts = [pltpu.make_async_copy(a, b, in_sem.at[i]) for i, (a, b) in enumerate(
        ((ids_in, ids), (slot_in, slot), (tok_in, tok), (gate_in, gate)))]
    for cp in firsts:
        cp.start()
    loads = []
    for r in range(PEERS):
        j = peer_index(r)
        for h in range(2):
            loads.append(pltpu.make_async_copy(
                w_in.at[0, pl.ds(pl.multiple_of(j * 256 + h * 128, 128), 128), :],
                w1.at[h, pl.ds(r * 128, 128), :], w_sem.at[len(loads)]))
        loads.append(pltpu.make_async_copy(
            w_out.at[0, :, pl.ds(pl.multiple_of(j * 256, 256), 256)],
            w2.at[r], w_sem.at[len(loads)]))
    for c in loads:
        c.start()

    for cp in firsts:
        cp.wait()
    e = ids[...]
    dz = (e // 4 - z + NZ) % NZ
    k = jnp.zeros_like(e)
    for d, s in SLOT_OF.items():
        k = jnp.where(dz == d, s, k)
    sub = ((e // 2 % 2 + ylo) % 2) * 2 + (e % 2 + core) % 2
    c = slot[...]
    half_k = k // (NZ // 2)
    target = jnp.where(c >= 0, (half_k * SUB + sub - half_k) * HALF + k * CAP + c, -1)
    rows = lax.broadcasted_iota(jnp.int32, (SUB * NZ * CAP, 256), 0)
    chosen = (rows == target[0:1, :]) | (rows == target[1:2, :])
    panel = jnp.dot(chosen.astype(F32).astype(BF), tok[...], preferred_element_type=F32)
    near_out[...] = panel.astype(BF).reshape(2, SUB, HALF, 256)

    pl.semaphore_wait(barrier, len(partners))

    near = []
    for half in range(2):
        for i in range(1, SUB):
            cp = remote(near_out.at[half, i], near_in.at[half, i], near_s.at[half, i],
                        near_r.at[half, i], at_sub(i))
            cp.start()
            near.append(cp)
    near_in[:, 0] = near_out[:, 0]

    def near_of_far(i, swap):
        kk = (i * 1639) >> 16
        rest = i - kk * 40
        if swap:
            kk = kk + 1 - 2 * (kk % 2)
        ss = (rest * 205) >> 11
        return ss * HALF + kk * CAP + rest - ss * 10

    n = SUB * HALF
    near_cols = lax.broadcasted_iota(jnp.int32, (n, n), 1)
    near_rows = lax.broadcasted_iota(jnp.int32, (n, n), 0)
    far_rows = lax.broadcasted_iota(jnp.int32, (n, 1), 0)
    far_cols = lax.broadcasted_iota(jnp.int32, (1, n), 1)
    for h in range(2):
        mix[h] = (near_of_far(far_rows, h) == near_cols).astype(F32).astype(BF)

    upper = lax.broadcasted_iota(jnp.int32, (2 * UNIT, 128), 0) < UNIT

    def pick(a, b):
        return jnp.where(upper, a, b)

    far = {}

    def arrange(half):
        for cp in near[half * 3:half * 3 + 3]:
            cp.wait_recv()
        arrived = near_in[half].reshape(n, 256)
        order0 = jnp.dot(mix[0], arrived[:, :128], preferred_element_type=F32)
        order1 = jnp.dot(mix[1], arrived[:, 128:], preferred_element_type=F32)
        for k in range(NZ // 2):
            s = half * (NZ // 2) + k
            a = order0[(k // 2) * 80:(k // 2 + 1) * 80]
            b = order1[(k // 2) * 80:(k // 2 + 1) * 80]
            block = (pick(a, b) if s % 2 == 0 else pick(b, a)).astype(BF)
            if DZ[s] == 0:
                far_in[0, s] = block
            else:
                far_out[s] = block

    def spread(g):
        for s in range(g * 4, g * 4 + 4):
            if DZ[s]:
                far[s] = remote(far_out.at[s], far_in.at[0, BACK[s]], far_s.at[s],
                                far_r.at[BACK[s]], at_z(DZ[s]))
                far[s].start()

    def drain(g):
        for s in range(g * 4, g * 4 + 4):
            if DZ[s]:
                far[s].wait_send()

    def prepare(_):
        for h in range(2):
            unmix[h] = (near_of_far(far_cols, h) == near_rows).astype(F32).astype(BF)
        g = gate[...]
        weighted = jnp.where(rows == target[0:1, :], g[0:1, :], 0.0) + jnp.where(
            rows == target[1:2, :], g[1:2, :], 0.0)
        hi = weighted.astype(BF)
        lo = weighted - hi.astype(F32)
        for half in range(2):
            gates_hi[half] = hi[half * n:(half + 1) * n].astype(F32).T.astype(BF)
            gates_lo[half] = lo[half * n:(half + 1) * n].T.astype(BF)

    def loaded(_):
        for cp in loads:
            cp.wait()

    sent = {}
    backs = []
    H = PER // 2

    def send(g, kind, i, src, dst, to):
        n = FIRST[kind] + i
        cp = remote(src, dst, tree_s.at[g, n], tree_r.at[g, n], at_peer(to))
        cp.start()
        sent[g, kind, i] = cp

    def got(g, kind, *which):
        for i in which:
            sent[g, kind, i].wait_recv()

    def part(g, half):
        return pl.ds(g * PER + half * H, H)

    def gather0(g):
        for s in range(g * PER, (g + 1) * PER):
            if DZ[s]:
                remote(far_out.at[s], far_in.at[0, s], far_s.at[s], far_r.at[s], at_z(DZ[s])).wait_recv()
        for kind in ("own", "rest"):
            for r in (ROW, 1, 3, 2):
                back = r if r == ROW else 4 - r
                piece = part(g, int((r == ROW) == (kind == "rest")))
                send(g, kind, back, far_in.at[0, piece], far_in.at[back, piece], r)

    def gather1(g):
        got(g, "own", ROW)
        for r in (1, 3, 2):
            send(g, "row", 4 - r, far_in.at[ROW, part(g, 0)], far_in.at[ROW + 4 - r, part(g, 0)], r)
        for r in (1, 3, 2):
            got(g, "own", r)
            send(g, "col", r, far_in.at[r, part(g, 1)], far_in.at[ROW + r, part(g, 1)], ROW)

    def compute(g):
        got(g, "rest", 1, 2, 3, ROW)
        got(g, "row", 1, 2, 3)
        got(g, "col", 1, 2, 3)
        left0, left1 = [], []
        for q in range(H):
            s = g * PER + 2 * q
            a0 = [far_in[r, s] for r in range(PEERS)]
            a1 = [far_in[r, s + 1] for r in range(PEERS)]
            left0.append(jnp.concatenate([pick(u, v) for u, v in zip(a0, a1)], axis=1))
            left1.append(jnp.concatenate([pick(v, u) for u, v in zip(a0, a1)], axis=1))
        acc0 = jnp.dot(jnp.concatenate(left0, axis=0), w1[0], preferred_element_type=F32)
        acc1 = jnp.dot(jnp.concatenate(left1, axis=0), w1[1], preferred_element_type=F32)
        swapped = []
        for q in range(H):
            swapped += [acc1[q * 80 + 40:q * 80 + 80], acc1[q * 80:q * 80 + 40]]
        v = acc0 + jnp.concatenate(swapped, axis=0)
        inner = 0.7978845608028654 * (v + 0.044715 * (v * v * v))
        hidden = (0.5 * v * (1.0 + jnp.tanh(inner))).astype(BF)
        for r in (5, 7, 6, 1, 3, 2, 4, 0):
            res = jnp.dot(hidden, w2[r], preferred_element_type=F32)
            for q in range(H):
                p0 = res[q * 80:q * 80 + 80, :128]
                p1 = res[q * 80:q * 80 + 80, 128:]
                p1 = jnp.concatenate([p1[40:], p1[:40]], axis=0)
                s = g * PER + 2 * q
                part_out[r // 4, r % 4, s] = pick(p0, p1).astype(BF)
                part_out[r // 4, r % 4, s + 1] = pick(p1, p0).astype(BF)
            if r in (1, 2, 3):
                send(g, "px", 4 - r, part_out.at[:, r, part(g, 0)], by_x.at[g, 4 - r], r)
            if r >= ROW:
                send(g, "py", r - ROW, part_out.at[1, r - ROW, part(g, 1)], by_y.at[g, r - ROW], ROW)

    def scatter1(g):
        for r in (1, 3, 2):
            got(g, "py", r)
            for i in range(H):
                s = g * PER + H + i
                part_out[0, r, s] = (part_out[0, r, s].astype(F32) + by_y[g, r, i].astype(F32)).astype(BF)
            send(g, "qx", 4 - r, part_out.at[0, r, part(g, 1)], last_x.at[g, 4 - r], r)
        got(g, "px", 1, 2, 3)
        for i in range(H):
            s = g * PER + i
            total = part_out[1, 0, s].astype(F32)
            for r in (1, 2, 3):
                total = total + by_x[g, r, 1, i].astype(F32)
            part_out[1, 0, s] = total.astype(BF)
        send(g, "qy", 0, part_out.at[1, 0, part(g, 0)], last_y.at[g], ROW)

    def give_back(s, value):
        if DZ[s] == 0:
            back_in[s] = value.astype(BF)
            return
        back_out[s] = value.astype(BF)
        cp = remote(back_out.at[s], back_in.at[BACK[s]], back_s.at[s], back_r.at[BACK[s]],
                    at_z(DZ[s]))
        cp.start()
        backs.append(cp)

    def finish(g):
        got(g, "qy", 0)
        for i in range(H):
            s = g * PER + i
            total = part_out[0, 0, s].astype(F32) + last_y[g, i].astype(F32)
            for r in (1, 2, 3):
                total = total + by_x[g, r, 0, i].astype(F32)
            give_back(s, total)
        got(g, "py", 0)
        got(g, "qx", 1, 2, 3)
        for i in range(H):
            s = g * PER + H + i
            total = part_out[0, 0, s].astype(F32) + by_y[g, 0, i].astype(F32)
            for r in (1, 2, 3):
                total = total + last_x[g, r, i].astype(F32)
            give_back(s, total)

    last = []

    def returned(half):
        for s in range(half * NZ // 2, (half + 1) * NZ // 2):
            if DZ[s]:
                remote(back_out.at[s], back_in.at[s], back_s.at[s], back_r.at[s],
                       at_z(DZ[s])).wait_recv()
        left0, left1 = [], []
        for q in range(half * NZ // 4, (half + 1) * NZ // 4):
            a, b = back_in[2 * q], back_in[2 * q + 1]
            left0.append(pick(a, b))
            left1.append(pick(b, a))
        res0 = jnp.dot(unmix[0], jnp.concatenate(left0, axis=0), preferred_element_type=F32)
        res1 = jnp.dot(unmix[1], jnp.concatenate(left1, axis=0), preferred_element_type=F32)
        res = jnp.concatenate([res0, res1], axis=1).astype(BF)
        last_in[half, 0] = res[:HALF]
        for i in range(1, SUB):
            last_out[half, i] = res[i * HALF:(i + 1) * HALF]
            cp = remote(last_out.at[half, i], last_in.at[half, i], last_s.at[half, i],
                        last_r.at[half, i], at_sub(i))
            cp.start()
            last.append(cp)

    sums = []

    def combine(half):
        for cp in last[half * 3:half * 3 + 3]:
            cp.wait_recv()
        rows_in = last_in[half].reshape(n, 256)
        sums.append(jnp.dot(gates_hi[half], rows_in, preferred_element_type=F32)
                    + jnp.dot(gates_lo[half], rows_in, preferred_element_type=F32))

    steps = {"m": arrange, "z": spread, "x": drain, "u": prepare, "w": loaded,
             "a": gather0, "b": gather1, "d": compute, "e": scatter1, "g": finish,
             "k": returned, "c": combine}
    for step, i in ORDER:
        steps[step](i)
    out[...] = (sums[0] + sums[1]).astype(BF)
    for cp in near + list(sent.values()) + backs + last:
        cp.wait_send()


def body(tokens, gate_values, expert_ids, slot_index, w_in, w_out):
    n = SUB * NZ * CAP
    vm = pl.BlockSpec(memory_space=pltpu.VMEM)
    hbm = pl.BlockSpec(memory_space=pl.ANY)
    dma = pltpu.SemaphoreType.DMA
    blocks = (NZ, 2 * UNIT, 128)
    return pl.pallas_call(
        kernel,
        out_shape=jax.ShapeDtypeStruct((256, 256), BF),
        in_specs=[hbm] * 6,
        out_specs=vm,
        scratch_shapes=[
            pltpu.VMEM((256, 256), BF), pltpu.VMEM((2, 256), jnp.int32),
            pltpu.VMEM((2, 256), jnp.int32), pltpu.VMEM((2, 256), F32), dma((4,)),
            pltpu.VMEM((2, 1024, 512), BF), pltpu.VMEM((PEERS, 512, 256), BF),
            pltpu.VMEM((2, n // 2, n // 2), BF), pltpu.VMEM((2, n // 2, n // 2), BF),
            pltpu.VMEM((2, 256, n // 2), BF), pltpu.VMEM((2, 256, n // 2), BF),
            pltpu.VMEM((2, SUB, HALF, 256), BF), pltpu.VMEM((2, SUB, HALF, 256), BF),
            pltpu.VMEM(blocks, BF), pltpu.VMEM((PEERS,) + blocks, BF),
            pltpu.VMEM((2, 4) + blocks, BF),
            pltpu.VMEM((GROUPS, 4, 2, PER // 2) + blocks[1:], BF),
            pltpu.VMEM((GROUPS, 4, PER // 2) + blocks[1:], BF),
            pltpu.VMEM((GROUPS, 4, PER // 2) + blocks[1:], BF),
            pltpu.VMEM((GROUPS, PER // 2) + blocks[1:], BF),
            pltpu.VMEM(blocks, BF), pltpu.VMEM(blocks, BF),
            pltpu.VMEM((2, SUB, HALF, 256), BF), pltpu.VMEM((2, SUB, HALF, 256), BF),
            dma((3 * PEERS,)), dma((2, SUB)), dma((2, SUB)), dma((NZ,)), dma((NZ,)),
            dma((GROUPS, 31)), dma((GROUPS, 31)),
            dma((NZ,)), dma((NZ,)), dma((2, SUB)), dma((2, SUB)),
        ],
        compiler_params=pltpu.CompilerParams(
            collective_id=0, has_side_effects=True, vmem_limit_bytes=60 * 2**20),
        name="moe",
    )(tokens, expert_ids.T, slot_index.T, gate_values.T, w_in, w_out)


def solution(mesh):
    placed = (
        P("expert", "tensor"),
        P("expert", None),
        P("expert", None),
        P("expert", None),
        P("expert", None, "tensor"),
        P("expert", "tensor", None),
    )
    return jax.shard_map(
        body, mesh=mesh, in_specs=placed, out_specs=P("expert", "tensor"), check_vma=False
    )
```
